256 devices in a mesh: dp: 2 (over x_lo), seq: 16 (over z, core), fsdp: 8 (over x_hi, y).
Axes of the slice: x: 4 (x_hi: 2, x_lo: 2; x = x_hi * 2 + x_lo), y: 4, z: 8, core: 2. Of those that a mesh axis runs over, the one named last changes fastest.
Arguments:
- queries_raw: bfloat16 [16, 4096, 2048], P(('dp', 'fsdp'), 'seq'), parts along dimension 0, may hold values from -6 to 6
- keys_values: bfloat16 [16, 4096, 2048], P(('dp', 'fsdp'), 'seq'), parts along dimension 0, may hold values from -6 to 6
- doc_ids: int32 [16, 4096], P(('dp', 'fsdp')), parts along dimension 0, may hold values from 0 to 3, never falling along the last dimension, each value on 1 to 2048 neighbouring positions
- q_gain: float32 [128], replicated, may hold values from 0.6 to 7
- k_gain: float32 [128], replicated, may hold values from 0.6 to 7
- out_weight: bfloat16 [2048, 5376], P('fsdp'), may hold values from -0.125 to 0.125
- post_gain: float32 [5376], replicated, may hold values from 0.25 to 1.75
Outputs:
- layer_out: bfloat16 [16, 4096, 5376], P(('dp', 'fsdp'), 'seq'), parts along dimension 0
The draws below stay inside these ranges and needn't reach their ends.
There are 2 independent parts, one for each index of `dp`. The reference program is written for one: setup_inputs(seed, part) draws one part's arguments, and reference() takes and returns one part's arrays. A program takes and returns all parts, laid end to end along the dimension named above; an argument that names none is the same for every part. Nothing has to cross between parts.
Inputs may be any that keep to these rules, and one draw needn't show every extreme that they name: `doc_ids`: each slab's document numbers never fall; a document has at most 2048 tokens, and one has exactly that many.
All inputs are finite; a program needn't handle non-finite values.
Results may differ from the reference program's by a relative error of at most 0.008.
The reference program's roundings to bfloat16 on the way (of `probs` and `attended`) count: a program that leaves them out, or rounds other values in their place, can miss the bound.
Values may be sent and summed in bfloat16 or wider, within the bound.
No kernel may reach another device: no remote copies, remote signals or barrier semaphores. Data moves between devices by JAX's collectives and lax.ppermute only.
A program may use at most 128 MiB of HBM per device.

```python
import math
import jax
import jax.numpy as jnp
import numpy as np
from jax import lax

D = 5376
HEADS = 16
KV_HEADS = 8
HEAD_DIM = 128
WINDOW = 1024
T_DEV = 256
FEAT = 2048
SLABS = 8
SLAB = 4096
DOCS = 4


def joint_draw(key):
    base_key = jax.random.fold_in(key, 4242)
    key_q, key_k, key_v = jax.random.split(base_key, 3)
    q_shape = (SLABS, SLAB, HEADS, HEAD_DIM)
    kv_shape = (SLABS, SLAB, KV_HEADS, HEAD_DIM)
    queries = jnp.clip(jax.random.normal(key_q, q_shape, jnp.float32), -6.0, 6.0)
    keys = jnp.clip(jax.random.normal(key_k, kv_shape, jnp.float32), -6.0, 6.0)
    values = jnp.clip(jax.random.normal(key_v, kv_shape, jnp.float32), -6.0, 6.0)
    joined = jnp.concatenate([keys.reshape(SLABS, SLAB, KV_HEADS * HEAD_DIM), values.reshape(SLABS, SLAB, KV_HEADS * HEAD_DIM)], axis=-1)
    return (queries.reshape(SLABS, SLAB, HEADS * HEAD_DIM), joined)


def draw_queries_raw(key, part):
    return joint_draw(key)[0].astype(jnp.bfloat16)


def draw_keys_values(key, part):
    return joint_draw(key)[1].astype(jnp.bfloat16)


def gain_draw(key):
    return jax.random.uniform(key, (HEAD_DIM,), jnp.float32, 0.6, 1.6)


def draw_q_gain(key, part):
    return gain_draw(jax.random.fold_in(key, 31))


def draw_k_gain(key, part):
    return gain_draw(jax.random.fold_in(key, 37))


def levels(own_key, shape, pieces, low, largest):
    factor_of, own = 1.0, jax.random.fold_in(own_key, 6)
    for axis_at, blocks in pieces:
        heights = jnp.exp(jax.random.uniform(jax.random.fold_in(own, axis_at), (blocks,), jnp.float32, low / len(pieces), largest / len(pieces)))
        factor_of = factor_of * jnp.repeat(heights, shape[axis_at] // blocks).reshape([-1 if axis == axis_at else 1 for axis in range(len(shape))])
    return factor_of


def split_up(number_of, total, most, slope):
    portions = [(1 << 20) // math.isqrt(grade ** slope) + 1 for grade in range(2, number_of + 1)]
    rest, holding = total - most - (number_of - 1), [1] * (number_of - 1)
    while rest > 0:
        free = [i for i in range(number_of - 1) if holding[i] < most]
        mass, remaining = sum([portions[i] for i in free]), rest
        for i in free:
            extra = min(most - holding[i], max(1, remaining * portions[i] // mass), rest)
            holding[i] = holding[i] + extra
            rest = rest - extra
    return np.array([most] + holding)


def ragged_sizes(key, number_of, total, bound, skew):
    if number_of == 2:
        one = jax.random.randint(key, (), max(1, total - bound), min(bound, total - 1) + 1)
        return jnp.stack([one, total - one])
    tallies = jnp.asarray(split_up(number_of, total, bound, skew), jnp.int32)
    couples = (number_of - 1) // 2
    donor, taker = tallies[1:1 + 2 * couples:2], tallies[2:2 + 2 * couples:2]
    margin = jnp.minimum(donor - 1, bound - taker)
    passed = jax.random.randint(jax.random.fold_in(key, 1), (couples,), 0, 1 << 20) % (margin + 1)
    tallies = tallies.at[1:1 + 2 * couples:2].set(donor - passed).at[2:2 + 2 * couples:2].set(taker + passed)
    return tallies[jax.random.permutation(jax.random.fold_in(key, 2), number_of)]


def centred(key, extent, spread, limit, shards=(), kind=jnp.bfloat16):
    factor_of = levels(key, extent, shards, -0.22, 0.18) if shards else 1.0
    drawn = jax.random.normal(key, extent, jnp.float32) * spread * factor_of
    return jnp.minimum(jnp.maximum(drawn, -limit), limit).astype(kind)


def setup_inputs(seed: int = 0, part: int = 0) -> dict:
    arg_keys = jax.random.split(jax.random.key(seed), 8)
    part_splits = jax.random.split(jax.random.fold_in(arg_keys[7], part), 8)
    queries_raw = draw_queries_raw(jax.random.fold_in(jax.random.fold_in(arg_keys[7], part), 71), part)
    keys_values = draw_keys_values(jax.random.fold_in(jax.random.fold_in(arg_keys[7], part), 71), part)
    doc_ids = jax.vmap(lambda own: jnp.searchsorted(jnp.cumsum(ragged_sizes(own, DOCS, SLAB, 2 * WINDOW, 2)), jnp.arange(SLAB), side="right"))(jax.random.split(part_splits[2], SLABS)).reshape((SLABS, SLAB)).astype(jnp.int32)
    q_gain = draw_q_gain(jax.random.fold_in(arg_keys[7], 71), part)
    k_gain = draw_k_gain(jax.random.fold_in(arg_keys[7], 71), part)
    out_weight = centred(arg_keys[5], (FEAT, D), FEAT ** -0.5, 0.125, ((0, 8),))
    post_gain = jnp.clip(1.0 + 0.15 * jax.random.normal(arg_keys[6], (D,), jnp.float32), 0.25, 1.75)
    return {"queries_raw": queries_raw, "keys_values": keys_values, "doc_ids": doc_ids, "q_gain": q_gain, "k_gain": k_gain, "out_weight": out_weight, "post_gain": post_gain}


attn_scale = 168.0 ** (-0.5)
norm_eps = 1e-06

def doc_positions(ids):
    count = ids.shape[0]
    index = jnp.arange(count, dtype=jnp.int32)
    flags = jnp.concatenate([jnp.ones((1,), bool), ids[1:] != ids[:-1]])
    starts = lax.cummax(jnp.where(flags, index, 0).astype(jnp.int32), axis=0)
    return (index - starts).astype(jnp.int32)

def norm_rope(inputs, gain, positions):
    values = inputs.astype(jnp.float32)
    meansq = lax.optimization_barrier(jnp.mean(values * values, axis=-1, keepdims=True))
    scaled = values * lax.rsqrt(meansq + norm_eps) * gain
    width = values.shape[-1]
    half = width // 2
    inverse = 10000.0 ** (-(jnp.arange(half, dtype=jnp.float32) * 2.0 / width))
    angles = positions.astype(jnp.float32)[:, None] * inverse[None, :]
    cosine = jnp.cos(angles)[:, None, :]
    sine = jnp.sin(angles)[:, None, :]
    first = scaled[..., :half]
    second = scaled[..., half:]
    rotated = jnp.concatenate([first * cosine - second * sine, second * cosine + first * sine], axis=-1)
    return rotated.astype(jnp.bfloat16)

def attend(queries, keys, values, allowed):
    scores = jnp.einsum('tkgd,ukd->kgtu', queries.astype(jnp.float32), keys.astype(jnp.float32)) * attn_scale
    scores = jnp.where(allowed[None, None], scores, -jnp.inf)
    top = lax.optimization_barrier(jnp.max(scores, axis=-1, keepdims=True))
    expd = jnp.exp(scores - top)
    total = lax.optimization_barrier(jnp.sum(expd, axis=-1, keepdims=True))
    probs = (expd / total).astype(jnp.bfloat16)
    mixed = jnp.einsum('kgtu,ukd->tkgd', probs.astype(jnp.float32), values.astype(jnp.float32))
    return mixed.reshape(queries.shape[0], -1).astype(jnp.bfloat16)

def reference(queries_raw, keys_values, doc_ids, q_gain, k_gain, out_weight, post_gain):
    group = HEADS // KV_HEADS
    kv_cols = KV_HEADS * HEAD_DIM

    def one_slab(operands):
        raw_q, raw_kv, ids = operands
        positions = doc_positions(ids)
        queries = norm_rope(raw_q.reshape(SLAB, HEADS, HEAD_DIM), q_gain, positions)
        keys = norm_rope(raw_kv[:, :kv_cols].reshape(SLAB, KV_HEADS, HEAD_DIM), k_gain, positions)
        values = raw_kv[:, kv_cols:].reshape(SLAB, KV_HEADS, HEAD_DIM)
        keys_pad = jnp.concatenate([jnp.zeros((WINDOW, KV_HEADS, HEAD_DIM), jnp.bfloat16), keys], axis=0)
        values_pad = jnp.concatenate([jnp.zeros((WINDOW, KV_HEADS, HEAD_DIM), jnp.bfloat16), values], axis=0)
        ids_pad = jnp.concatenate([jnp.full((WINDOW,), -1, jnp.int32), ids.astype(jnp.int32)])

        def one_block(block):
            start = (block * T_DEV).astype(jnp.int32)
            q_block = lax.dynamic_slice_in_dim(queries, start, T_DEV, 0).reshape(T_DEV, KV_HEADS, group, HEAD_DIM)
            k_block = lax.dynamic_slice_in_dim(keys_pad, start, T_DEV + WINDOW, 0)
            v_block = lax.dynamic_slice_in_dim(values_pad, start, T_DEV + WINDOW, 0)
            key_ids = lax.dynamic_slice_in_dim(ids_pad, start, T_DEV + WINDOW, 0)
            query_ids = lax.dynamic_slice_in_dim(ids.astype(jnp.int32), start, T_DEV, 0)
            relative = WINDOW + jnp.arange(T_DEV, dtype=jnp.int32)[:, None] - jnp.arange(T_DEV + WINDOW, dtype=jnp.int32)[None, :]
            allowed = (relative >= 0) & (relative < WINDOW) & (query_ids[:, None] == key_ids[None, :])
            attended = attend(q_block, k_block, v_block, allowed)
            projected = jnp.dot(attended, out_weight, preferred_element_type=jnp.float32)
            meansq = lax.optimization_barrier(jnp.mean(projected * projected, axis=-1, keepdims=True))
            return (projected * lax.rsqrt(meansq + norm_eps) * post_gain).astype(jnp.bfloat16)
        blocks = lax.map(one_block, jnp.arange(SLAB // T_DEV, dtype=jnp.int32))
        return blocks.reshape(SLAB, D)
    return lax.map(one_slab, (queries_raw, keys_values, doc_ids))
```

```python
import functools
import math

import jax
import jax.numpy as jnp
from jax import lax
from jax.experimental import pallas as pl
from jax.experimental.pallas import tpu as pltpu
from jax.sharding import PartitionSpec as P

WINDOW = 1024
NEG = -1e30
attn_scale = 168.0 ** (-0.5)
norm_eps = 1e-06
SCORE_MUL = attn_scale * math.log2(math.e)
LIMIT = 60 * 1024 * 1024

def vmem(n):
    return [pl.BlockSpec(memory_space=pltpu.VMEM)] * n


def call(body, out_shape, args, scalars=(), scratch=(), flops=0, nbytes=0):
    specs = [pl.BlockSpec(memory_space=pltpu.SMEM)] * len(scalars) + vmem(len(args))
    return pl.pallas_call(
        body,
        out_shape=out_shape,
        in_specs=specs,
        out_specs=jax.tree.map(lambda _: pl.BlockSpec(memory_space=pltpu.VMEM), out_shape),
        scratch_shapes=list(scratch),
        compiler_params=pltpu.CompilerParams(vmem_limit_bytes=LIMIT),
        cost_estimate=pl.CostEstimate(flops=flops, bytes_accessed=nbytes, transcendentals=0),
    )(*scalars, *args)


def rope_head(x, gain, cosd, sind):
    x = x.astype(jnp.float32)
    meansq = jnp.mean(x * x, axis=-1, keepdims=True)
    y = x * lax.rsqrt(meansq + norm_eps) * gain
    half = y.shape[-1] // 2
    rolled = jnp.concatenate([y[:, half:], y[:, :half]], axis=-1)
    return (y * cosd + rolled * sind).astype(jnp.bfloat16)


def prep_keys(kv_ref, gain_ref, cos_ref, sin_ref, k0_ref, k1_ref):
    hd = gain_ref.shape[1]
    part = k0_ref.shape[1]
    for i, out in enumerate((k0_ref, k1_ref)):
        for at in range(0, part, hd):
            out[:, at : at + hd] = rope_head(
                kv_ref[:, i * part + at : i * part + at + hd], gain_ref[...], cos_ref[...], sin_ref[...]
            )


def prep_queries(q_ref, gain_ref, cos_ref, sin_ref, q0_ref, q1_ref):
    hd = gain_ref.shape[1]
    tokens = q_ref.shape[0]
    n = q_ref.shape[1] // hd // 2
    for h in range(2 * n):
        out = (q0_ref, q1_ref)[h // n]
        out[h % n // 2, (h % 2) * tokens : (h % 2 + 1) * tokens, :] = rope_head(
            q_ref[:, h * hd : (h + 1) * hd], gain_ref[...], cos_ref[...], sin_ref[...]
        )


def attend(first, info, q_ref, lb_ref, *refs):
    keys, values = refs[:6], refs[6:12]
    out_ref, k_rest, v_rest = refs[12:]
    tokens, part = keys[0].shape
    hd = q_ref.shape[2]
    begin, core = info[0], info[1]

    @pl.when(core == 0)
    def _():
        k_rest[...] = keys[4][...]
        v_rest[...] = values[4][:, first : first + part]

    @pl.when(core != 0)
    def _():
        k_rest[...] = keys[5][...]
        v_rest[...] = values[5][:, first : first + part]

    lb = jnp.concatenate([lb_ref[...], lb_ref[...]], axis=0)
    rows = lax.broadcasted_iota(jnp.int32, (2 * tokens, tokens), 0)
    cols = lax.broadcasted_iota(jnp.int32, (2 * tokens, tokens), 1)
    ones = jnp.ones((tokens, hd), jnp.bfloat16)
    blocks = (
        (keys[0], values[0], first, begin),
        (keys[1], values[1], first, begin - 2 * tokens),
        (keys[2], values[2], first, begin - jnp.where(core == 0, 1, 3) * tokens),
        (k_rest, v_rest, 0, begin - jnp.where(core == 0, 3, 1) * tokens),
        (keys[3], values[3], first, begin - 4 * tokens),
    )
    causal = cols <= lax.rem(rows, tokens)
    for j in range(out_ref.shape[0]):
        at = j * hd
        q = q_ref[j]
        scores = []
        for i, (k, _, _, base) in enumerate(blocks):
            s = lax.dot_general(
                q, k[:, at : at + hd], (((1,), (1,)), ((), ())), preferred_element_type=jnp.float32
            )
            keep = cols >= lb - base
            if i == 0:
                keep = keep & causal
            scores.append(jnp.where(keep, s * SCORE_MUL, NEG))
        top = functools.reduce(jnp.maximum, scores)
        top = jnp.max(top, axis=-1, keepdims=True)
        acc = jnp.zeros((2 * tokens, 2 * hd), jnp.float32)
        for s, (_, values_ref, lo, _) in zip(scores, blocks):
            v = values_ref[:, lo + at : lo + at + hd]
            acc += jnp.dot(
                jnp.exp2(s - top).astype(jnp.bfloat16),
                jnp.concatenate([v, ones], axis=1),
                preferred_element_type=jnp.float32,
            )
        mixed = (acc[:, :hd] / acc[:, hd:]).astype(jnp.bfloat16)
        out_ref[j, :, :hd] = mixed[:tokens]
        out_ref[j, :, hd:] = mixed[tokens:]


def pieces(dp, core):
    up, down = (1, 2) if dp else (2, 1)
    first = [("own.a", 0), ("own.b", 0)], [("y0.0", up), ("y0.1", down)], [("y1.0", up), ("y1.1", down)]
    far = [("y2.0", 3)], [("y2.1", 3)]
    ring = [("x1.0", 4)], [("x0.1", 4)]
    left = first[0][:1] + first[1] + far[1 - dp] + ring[1 - dp] + [("x1.1", 4 + down), ("x2.0", 4 + up)]
    right = first[0][1:] + first[2] + far[dp] + ring[dp] + [("x2.1", 4 + down)]
    late = [("y3.0", 7)], [("x3.0", 4 + up), ("y3.1", 7)]

    def named(items):
        return [
            (n if n.startswith("own") else ("m." if int(n[-1]) == core else "p.") + n[:2], at) for n, at in items
        ]

    return (named(left), named(right)), (named(late[0]), named(late[1]))


EARLY = ("own.a", "own.b") + tuple(side + n for side in ("m.", "p.") for n in ("y0", "y1", "y2", "x0", "x1", "x2"))
LATE = ("m.y3", "m.x3", "p.y3", "p.x3")


def multiply(late, names, info, refs, att_ref, store):
    for core in range(2):
        for dp in range(2):

            @pl.when((info[0] == core) & (info[1] == dp))
            def _():
                for half, items in enumerate(pieces(dp, core)[late]):
                    wide = refs[0].shape[1]
                    for lo in range(0, wide, 256):
                        hi = min(lo + 256, wide)
                        total = None
                        for name, place in items:
                            x = jnp.dot(
                                att_ref[info[2 + place]],
                                refs[names.index(name)][:, lo:hi],
                                preferred_element_type=jnp.float32,
                            )
                            total = x if total is None else total + x
                        store(half, lo, hi, total)


def gather_heads(att0_ref, att1_ref, att_ref):
    @pl.when(pl.program_id(0) == 0)
    def _():
        n = att0_ref.shape[0]
        att_ref[:n] = att0_ref[...]
        att_ref[n:] = att1_ref[...]


def project_early(info, att0_ref, att1_ref, *refs):
    acc_ref, att_ref = refs[-2:]
    gather_heads(att0_ref, att1_ref, att_ref)

    def store(half, lo, hi, total):
        acc_ref[half, :, lo:hi] = total

    multiply(0, EARLY, info, refs, att_ref, store)


def project_late(info, att0_ref, att1_ref, gain_ref, early_ref, *refs):
    out_ref, att_ref, acc_ref, square_ref = refs[-4:]
    gather_heads(att0_ref, att1_ref, att_ref)
    i = pl.program_id(0)
    steps = pl.num_programs(0)
    rows, wide = early_ref.shape[1:]

    @pl.when(i == 0)
    def _():
        square_ref[...] = jnp.zeros_like(square_ref)

    def store(half, lo, hi, total):
        total = total + early_ref[half, :, lo:hi]
        acc_ref[half, i, :, lo:hi] = total
        squares = square_ref[...]
        for at in range(0, hi - lo, 128):
            x = total[:, at : at + 128]
            squares += x * x
        square_ref[...] = squares

    multiply(1, LATE, info, refs, att_ref, store)

    @pl.when(i == steps - 1)
    def _():
        cols = out_ref.shape[1]
        meansq = jnp.sum(square_ref[...], axis=-1, keepdims=True) / cols
        scale = lax.rsqrt(meansq + norm_eps)
        for half in range(2):
            for k in range(cols // 2 // wide):
                at = half * (cols // 2) + k * wide
                out_ref[:, at : at + wide] = (
                    acc_ref[half, k] * scale * gain_ref[:, at : at + wide]
                ).astype(jnp.bfloat16)


def on_device(queries_raw, keys_values, doc_ids, q_gain, k_gain, out_weight, post_gain):
    tokens, feat = queries_raw.shape[1:]
    head_dim = q_gain.shape[0]
    kv_cols = keys_values.shape[2] // 2
    kv_heads = kv_cols // head_dim
    n_seq = lax.axis_size("seq")
    n_fsdp = lax.axis_size("fsdp")
    n_y = n_fsdp // 2
    seq, fsdp, dp = lax.axis_index("seq"), lax.axis_index("fsdp"), lax.axis_index("dp")
    core = lax.rem(seq, 2)
    begin = seq * tokens
    f32 = jnp.float32

    forward = [(i, (i + 2) % n_seq) for i in range(n_seq)]
    across = [(i, i ^ 1) for i in range(n_seq)]
    everywhere = ("dp", "seq", "fsdp")

    def route(to):
        out = []
        for d in range(2):
            for q in range(n_seq):
                for f in range(n_fsdp):
                    e, r, g = to(d, q, f)
                    out.append(((d * n_seq + q) * n_fsdp + f, (e * n_seq + r) * n_fsdp + g))
        return out

    def y_to(d, q, f):
        step = 1 if q % 2 != d else -1
        return d, q, f // n_y * n_y + (f + step) % n_y

    def x_first_to(d, q, f):
        return 1 - d, q, (f + n_y) % n_fsdp if q % 2 else f

    def x_to(d, q, f):
        return 1 - d, q ^ 1, f if q % 2 else (f + n_y) % n_fsdp

    def along_y(x):
        return lax.ppermute(x, everywhere, route(y_to))

    def along_x_first(x):
        return lax.ppermute(x, everywhere, route(x_first_to))

    def along_x(x):
        return lax.ppermute(x, everywhere, route(x_to))

    def along_z(x):
        return lax.ppermute(x, "seq", forward)

    def swap(x):
        return lax.ppermute(x, "seq", across)

    ids = doc_ids[0]
    my_ids = lax.dynamic_slice_in_dim(ids, begin, tokens, 0)
    token = begin + jnp.arange(tokens, dtype=jnp.int32)
    start = jnp.sum((ids[None, :] < my_ids[:, None]).astype(jnp.int32), axis=1)
    positions = token - start
    lb = jnp.maximum(start, token - (WINDOW - 1))[:, None]
    half = head_dim // 2
    inverse = 10000.0 ** (-(jnp.arange(half, dtype=f32) * 2.0 / head_dim))
    angles = positions.astype(f32)[:, None] * inverse[None, :]
    cosine, sine = jnp.cos(angles), jnp.sin(angles)
    cosd = jnp.concatenate([cosine, cosine], axis=1)
    sind = jnp.concatenate([-sine, sine], axis=1)
    kg, qg = k_gain[None, :], q_gain[None, :]

    raw = keys_values[0]
    half_cols = out_weight.shape[1] // 2
    hold = lax.optimization_barrier
    info = jnp.stack([begin, core]).astype(jnp.int32)
    m, p = {}, {}

    v_own = raw[:, kv_cols:]
    v_near = along_z(v_own)
    sent, v_own = hold((out_weight, v_own))
    own_a = sent[:, :half_cols]
    m["y0"] = along_y(own_a)
    sent, own_a = hold((sent, own_a))
    own_b = sent[:, half_cols:]
    m["x0"] = along_x_first(jnp.where(dp == 0, own_b, own_a))
    shape = jax.ShapeDtypeStruct((tokens, kv_cols // 2), jnp.bfloat16)
    k_own = call(prep_keys, (shape, shape), (raw, kg, cosd, sind), flops=2 * 10**9, nbytes=2 * 10**6)
    k_near = [along_z(k_own[0])]
    m, v_own, v_near, k_own, k_near, own_b = hold((m, v_own, v_near, list(k_own), k_near, own_b))

    m["y1"] = along_y(own_b)
    m["x1"] = along_x(jnp.where(core == 0, m["y0"], m["x0"]))
    k_near.append(along_z(k_own[1]))
    v_far = along_z(v_near)
    late = (k_near[1], v_own, k_own, v_near, k_near[0], m["y0"], m["x0"])
    k_near[1], v_own, k_own, v_near, k_near[0], y0, x0 = hold(late)
    qshape = jax.ShapeDtypeStruct((kv_heads // 2, 2 * tokens, head_dim), jnp.bfloat16)
    qs = call(prep_queries, (qshape, qshape), (queries_raw[0], qg, cosd, sind), flops=3 * 10**9, nbytes=2 * 10**6)
    v_own_o, k_own_o = swap(v_own), [swap(k) for k in k_own]
    v_near_o, k_near_o = swap(v_near), [swap(k_near[0])]
    p["y0"], p["x0"] = swap(y0), swap(x0)
    state = (m, p, v_own, k_own, v_near, k_near, v_far, list(qs), v_own_o, k_own_o, v_near_o, k_near_o)
    m, p, v_own, k_own, v_near, k_near, v_far, qs, v_own_o, k_own_o, v_near_o, k_near_o = hold(state)

    m["y2"] = along_y(jnp.where(core != dp, m["y0"], m["y1"]))
    m["x2"] = along_x(jnp.where(core == 0, m["y1"], m["x1"]))
    k_far = [along_z(k) for k in k_near]
    k_far[0], near_1, y1, x1, v_far = hold((k_far[0], k_near[1], m["y1"], m["x1"], v_far))
    v_far_o, k_far_o = swap(v_far), [swap(k_far[0])]
    k_near_o.append(swap(near_1))
    p["y1"], p["x1"] = swap(y1), swap(x1)

    def attention(i):
        return call(
            functools.partial(attend, i * kv_cols // 2),
            jax.ShapeDtypeStruct((kv_heads // 2, tokens, 2 * head_dim), jnp.bfloat16),
            (
                qs[i], lb,
                k_own[i], k_near[i], k_near_o[i], k_far[i], k_far_o[i], k_own_o[i],
                v_own, v_near, v_near_o, v_far, v_far_o, v_own_o,
            ),
            scalars=(info,),
            scratch=(pltpu.VMEM((tokens, kv_cols // 2), jnp.bfloat16),) * 2,
            flops=8 * 10**9,
            nbytes=4 * 10**6,
        )

    att = [attention(0)]
    state = (m, p, k_near, k_far, k_near_o, v_far, v_far_o, att)
    m, p, k_near, k_far, k_near_o, v_far, v_far_o, att = hold(state)

    m["y3"] = along_y(m["x2"])
    m["x3"] = along_x(m["x2"])
    k_far_o.append(swap(k_far[1]))
    p["y2"], p["x2"] = swap(m["y2"]), swap(m["x2"])
    att.append(attention(1))
    g, y = fsdp // n_y, fsdp % n_y
    steps = [y, (y - 1) % n_y, (y + 1) % n_y, (y + 2) % n_y]
    shards = [x * n_y + at for x in (g, 1 - g) for at in steps]
    where = jnp.stack([core, dp, *shards]).astype(jnp.int32)
    w = {side + n: x for side, have in (("m.", m), ("p.", p)) for n, x in have.items()}

    tile = half_cols // 3
    n_tiles = half_cols // tile
    smem = pl.BlockSpec(memory_space=pltpu.SMEM)
    whole = pl.BlockSpec((kv_heads // 2, tokens, 2 * head_dim), lambda i: (0, 0, 0))
    column = pl.BlockSpec((out_weight.shape[0], tile), lambda i: (0, i))
    right = pl.BlockSpec((out_weight.shape[0], tile), lambda i: (0, n_tiles + i))
    early_block = pl.BlockSpec((2, tokens, tile), lambda i: (0, 0, i))
    heads = pltpu.VMEM((kv_heads, tokens, 2 * head_dim), jnp.bfloat16)
    early = pl.pallas_call(
        project_early,
        grid=(n_tiles,),
        out_shape=jax.ShapeDtypeStruct((2, tokens, half_cols), f32),
        in_specs=[smem, whole, whole, column, right] + [column] * (len(EARLY) - 2),
        out_specs=early_block,
        scratch_shapes=[heads],
        compiler_params=pltpu.CompilerParams(vmem_limit_bytes=LIMIT),
        cost_estimate=pl.CostEstimate(flops=5 * 10**9, bytes_accessed=24 * 10**6, transcendentals=0),
    )(where, *att, out_weight, out_weight, *[w[n] for n in EARLY[2:]])
    m, early = hold((m, early))

    w = {"m.y3": m["y3"], "m.x3": m["x3"], "p.y3": swap(m["y3"]), "p.x3": swap(m["x3"])}
    cols = 2 * half_cols
    out = pl.pallas_call(
        project_late,
        grid=(n_tiles,),
        out_shape=jax.ShapeDtypeStruct((tokens, cols), jnp.bfloat16),
        in_specs=[smem, whole, whole, pl.BlockSpec((1, cols), lambda i: (0, 0)), early_block]
        + [column] * len(LATE),
        out_specs=pl.BlockSpec((tokens, cols), lambda i: (0, 0)),
        scratch_shapes=[
            heads,
            pltpu.VMEM((2, n_tiles, tokens, tile), f32),
            pltpu.VMEM((tokens, 128), f32),
        ],
        compiler_params=pltpu.CompilerParams(vmem_limit_bytes=LIMIT),
        cost_estimate=pl.CostEstimate(flops=2 * 10**9, bytes_accessed=14 * 10**6, transcendentals=0),
    )(where, *att, post_gain[None, :], early, *[w[n] for n in LATE])
    return out[None]


def solution(mesh):
    in_specs = (
        P(("dp", "fsdp"), "seq", None),
        P(("dp", "fsdp"), "seq", None),
        P(("dp", "fsdp"), None),
        P(),
        P(),
        P("fsdp", None),
        P(),
    )
    out_specs = P(("dp", "fsdp"), "seq", None)
    return jax.shard_map(
        on_device, mesh=mesh, in_specs=in_specs, out_specs=out_specs, check_vma=False
    )
```

```python
import functools
import math

import jax
import jax.numpy as jnp
from jax import lax
from jax.experimental import pallas as pl
from jax.experimental.pallas import tpu as pltpu
from jax.sharding import PartitionSpec as P

WINDOW = 1024
NEG = -1e30
attn_scale = 168.0 ** (-0.5)
norm_eps = 1e-06
SCORE_MUL = attn_scale * math.log2(math.e)
MIB = 1024 * 1024
COST = pl.CostEstimate(flops=10**6, bytes_accessed=10**4, transcendentals=0)


def vmem(n):
    return [pl.BlockSpec(memory_space=pltpu.VMEM)] * n


def call(body, out_shape, args, scalars=(), scratch=(), limit=8):
    specs = [pl.BlockSpec(memory_space=pltpu.SMEM)] * len(scalars) + vmem(len(args))
    return pl.pallas_call(
        body,
        out_shape=out_shape,
        in_specs=specs,
        out_specs=jax.tree.map(lambda _: pl.BlockSpec(memory_space=pltpu.VMEM), out_shape),
        scratch_shapes=list(scratch),
        compiler_params=pltpu.CompilerParams(vmem_limit_bytes=limit * MIB),
        cost_estimate=COST,
    )(*scalars, *args)


def choose_kernel(flag, a_ref, b_ref, out_ref, sem):
    @pl.when(flag[0] != 0)
    def _():
        copy = pltpu.make_async_copy(a_ref, out_ref, sem)
        copy.start()
        copy.wait()

    @pl.when(flag[0] == 0)
    def _():
        copy = pltpu.make_async_copy(b_ref, out_ref, sem)
        copy.start()
        copy.wait()


def choose(flag, a, b):
    anywhere = pl.BlockSpec(memory_space=pl.ANY)
    return pl.pallas_call(
        choose_kernel,
        out_shape=jax.ShapeDtypeStruct(a.shape, a.dtype),
        in_specs=[pl.BlockSpec(memory_space=pltpu.SMEM), anywhere, anywhere],
        out_specs=pl.BlockSpec(memory_space=pltpu.VMEM),
        scratch_shapes=[pltpu.SemaphoreType.DMA],
        compiler_params=pltpu.CompilerParams(vmem_limit_bytes=4 * MIB),
        cost_estimate=COST,
    )(flag, a, b)


def rope_head(x, gain, cosd, sind):
    x = x.astype(jnp.float32)
    meansq = jnp.mean(x * x, axis=-1, keepdims=True)
    y = x * lax.rsqrt(meansq + norm_eps) * gain
    half = y.shape[-1] // 2
    rolled = jnp.concatenate([y[:, half:], y[:, :half]], axis=-1)
    return (y * cosd + rolled * sind).astype(jnp.bfloat16)


def prep_keys(kv_ref, gain_ref, cos_ref, sin_ref, k0_ref, k1_ref):
    hd = gain_ref.shape[1]
    part = k0_ref.shape[1]
    for i, out in enumerate((k0_ref, k1_ref)):
        for at in range(0, part, hd):
            out[:, at : at + hd] = rope_head(
                kv_ref[:, i * part + at : i * part + at + hd], gain_ref[...], cos_ref[...], sin_ref[...]
            )


def prep_queries(q_ref, gain_ref, cos_ref, sin_ref, q0_ref, q1_ref):
    hd = gain_ref.shape[1]
    tokens = q_ref.shape[0]
    n = q_ref.shape[1] // hd // 2
    for h in range(2 * n):
        out = (q0_ref, q1_ref)[h // n]
        out[h % n // 2, (h % 2) * tokens : (h % 2 + 1) * tokens, :] = rope_head(
            q_ref[:, h * hd : (h + 1) * hd], gain_ref[...], cos_ref[...], sin_ref[...]
        )


def attend(first, info, q_ref, lb_ref, *refs):
    keys, values = refs[:6], refs[6:12]
    out_ref, k_rest, v_rest = refs[12:]
    tokens, part = keys[0].shape
    hd = q_ref.shape[2]
    begin, core = info[0], info[1]

    @pl.when(core == 0)
    def _():
        k_rest[...] = keys[4][...]
        v_rest[...] = values[4][:, first : first + part]

    @pl.when(core != 0)
    def _():
        k_rest[...] = keys[5][...]
        v_rest[...] = values[5][:, first : first + part]

    lb = jnp.concatenate([lb_ref[...], lb_ref[...]], axis=0)
    rows = lax.broadcasted_iota(jnp.int32, (2 * tokens, tokens), 0)
    cols = lax.broadcasted_iota(jnp.int32, (2 * tokens, tokens), 1)
    ones = jnp.ones((tokens, hd), jnp.bfloat16)
    blocks = (
        (keys[0], values[0], first, begin),
        (keys[1], values[1], first, begin - 2 * tokens),
        (keys[2], values[2], first, begin - jnp.where(core == 0, 1, 3) * tokens),
        (k_rest, v_rest, 0, begin - jnp.where(core == 0, 3, 1) * tokens),
        (keys[3], values[3], first, begin - 4 * tokens),
    )
    causal = cols <= lax.rem(rows, tokens)
    for j in range(out_ref.shape[0]):
        at = j * hd
        q = q_ref[j]
        scores = []
        for i, (k, _, _, base) in enumerate(blocks):
            s = lax.dot_general(
                q, k[:, at : at + hd], (((1,), (1,)), ((), ())), preferred_element_type=jnp.float32
            )
            keep = cols >= lb - base
            if i == 0:
                keep = keep & causal
            scores.append(jnp.where(keep, s * SCORE_MUL, NEG))
        top = functools.reduce(jnp.maximum, scores)
        top = jnp.max(top, axis=-1, keepdims=True)
        acc = jnp.zeros((2 * tokens, 2 * hd), jnp.float32)
        for s, (_, values_ref, lo, _) in zip(scores, blocks):
            v = values_ref[:, lo + at : lo + at + hd]
            acc += jnp.dot(
                jnp.exp2(s - top).astype(jnp.bfloat16),
                jnp.concatenate([v, ones], axis=1),
                preferred_element_type=jnp.float32,
            )
        mixed = (acc[:, :hd] / acc[:, hd:]).astype(jnp.bfloat16)
        out_ref[j, :, :hd] = mixed[:tokens]
        out_ref[j, :, hd:] = mixed[tokens:]


def gather_heads(mine, other, att_ref):
    @pl.when(pl.program_id(0) == 0)
    def _():
        n, tokens = mine[0].shape[:2]
        for i in range(2):
            att_ref[i * n : (i + 1) * n, :tokens] = mine[i][...]
            att_ref[i * n : (i + 1) * n, tokens:] = other[i][...]


def multiply(items, extra, use_extra, info, att_ref, store):
    def run(items):
        wide = items[0][0].shape[1]
        for lo in range(0, wide, 256):
            hi = min(lo + 256, wide)
            total = None
            for ref, at in items:
                x = jnp.dot(att_ref[info[at]], ref[:, lo:hi], preferred_element_type=jnp.float32)
                total = x if total is None else total + x
            store(lo, hi, total)

    @pl.when(use_extra)
    def _():
        run(items + [extra])

    @pl.when(jnp.logical_not(use_extra))
    def _():
        run(items)


def project_early(info, m0, m1, o0, o1, own, y0, y1, y2, x0, x1, x2, acc_ref, att_ref):
    gather_heads((m0, m1), (o0, o1), att_ref)

    def store(lo, hi, total):
        acc_ref[:, lo:hi] = total

    items = [(own, 2), (y0, 3), (y1, 4), (y2, 5), (x1, 7), (x2, 8)]
    multiply(items, (x0, 6), info[0] == info[1], info, att_ref, store)


def project_late(info, m0, m1, o0, o1, early_ref, y3, x3, keep_ref, send_ref, *rest):
    sums, att_ref = rest[:2], rest[2]
    gather_heads((m0, m1), (o0, o1), att_ref)
    tokens = keep_ref.shape[0]

    @pl.when(pl.program_id(0) == 0)
    def _():
        for ref in sums:
            ref[...] = jnp.zeros_like(ref)

    def store(lo, hi, total):
        total = total + early_ref[:, lo:hi]
        keep_ref[:, lo:hi] = total[:tokens].astype(jnp.bfloat16)
        send_ref[:, lo:hi] = total[tokens:].astype(jnp.bfloat16)
        for i, ref in enumerate(sums):
            squares = ref[...]
            for at in range(0, hi - lo, 128):
                x = total[i * tokens : (i + 1) * tokens, at : at + 128]
                squares += x * x
            ref[...] = squares

    multiply([(y3, 9)], (x3, 10), info[0] != info[1], info, att_ref, store)


def norm_rows(info, keep_ref, came_ref, sum_ref, came_sum_ref, gain_ref, out_ref):
    half = keep_ref.shape[1]
    squares = jnp.sum(sum_ref[...] + came_sum_ref[...], axis=-1, keepdims=True)
    scale = lax.rsqrt(squares / (2 * half) + norm_eps)

    def write(at, ref):
        out_ref[:, at : at + half] = (
            ref[...].astype(jnp.float32) * scale * gain_ref[:, at : at + half]
        ).astype(jnp.bfloat16)

    for core in range(2):

        @pl.when(info[0] == core)
        def _():
            write(core * half, keep_ref)
            write((1 - core) * half, came_ref)


def on_device(queries_raw, keys_values, doc_ids, q_gain, k_gain, out_weight, post_gain):
    tokens, feat = queries_raw.shape[1:]
    head_dim = q_gain.shape[0]
    kv_cols = keys_values.shape[2] // 2
    kv_heads = kv_cols // head_dim
    n_seq = lax.axis_size("seq")
    n_fsdp = lax.axis_size("fsdp")
    n_y = n_fsdp // 2
    seq, fsdp, dp = lax.axis_index("seq"), lax.axis_index("fsdp"), lax.axis_index("dp")
    core = lax.rem(seq, 2)
    begin = seq * tokens
    f32 = jnp.float32

    forward = [(i, (i + 2) % n_seq) for i in range(n_seq)]
    across = [(i, i ^ 1) for i in range(n_seq)]
    everywhere = ("dp", "seq", "fsdp")

    def route(to):
        out = []
        for d in range(2):
            for q in range(n_seq):
                for f in range(n_fsdp):
                    e, r, g = to(d, q, f)
                    out.append(((d * n_seq + q) * n_fsdp + f, (e * n_seq + r) * n_fsdp + g))
        return out

    def turn(f, step):
        return f // n_y * n_y + (f + step) % n_y

    def y_out(d, q, f):
        return d, q, turn(f, -1 if q % 2 else 1)

    def y_back(d, q, f):
        return d, q, turn(f, 1 if q % 2 else -1)

    def x_to(d, q, f):
        return 1 - d, q, f if q % 2 == d else (f + n_y) % n_fsdp

    def move(x, to):
        return lax.ppermute(x, everywhere, route(to))

    def along_z(x):
        return lax.ppermute(x, "seq", forward)

    def swap(x):
        return lax.ppermute(x, "seq", across)

    ids = doc_ids[0]
    my_ids = lax.dynamic_slice_in_dim(ids, begin, tokens, 0)
    token = begin + jnp.arange(tokens, dtype=jnp.int32)
    start = jnp.sum((ids[None, :] < my_ids[:, None]).astype(jnp.int32), axis=1)
    positions = token - start
    lb = jnp.maximum(start, token - (WINDOW - 1))[:, None]
    half = head_dim // 2
    inverse = 10000.0 ** (-(jnp.arange(half, dtype=f32) * 2.0 / head_dim))
    angles = positions.astype(f32)[:, None] * inverse[None, :]
    cosine, sine = jnp.cos(angles), jnp.sin(angles)
    cosd = jnp.concatenate([cosine, cosine], axis=1)
    sind = jnp.concatenate([-sine, sine], axis=1)
    kg, qg = k_gain[None, :], q_gain[None, :]

    raw = keys_values[0]
    half_cols = out_weight.shape[1] // 2
    rows = out_weight.shape[0]
    hold = lax.optimization_barrier
    info = jnp.stack([begin, core]).astype(jnp.int32)
    same = core == dp
    flag = same.astype(jnp.int32)[None]

    own = lax.dynamic_slice(out_weight, (0, core * half_cols), (rows, half_cols))
    y0 = move(own, y_out)
    x0 = move(own, x_to)
    raw, own = hold((raw, own))
    v_own = raw[:, kv_cols:]
    v_near = along_z(v_own)
    shape = jax.ShapeDtypeStruct((tokens, kv_cols // 2), jnp.bfloat16)
    k_own = call(prep_keys, (shape, shape), (raw, kg, cosd, sind))
    k_near = [along_z(k_own[0])]
    v_near, v_own, k_own = hold((v_near, v_own, list(k_own)))
    v_own_o, k_own_o = swap(v_own), [swap(k) for k in k_own]
    state = (y0, x0, own, v_own, v_near, k_own, k_near, v_own_o, k_own_o)
    y0, x0, own, v_own, v_near, k_own, k_near, v_own_o, k_own_o = hold(state)

    y1 = move(own, y_back)
    x1 = move(choose(flag, x0, y0), x_to)
    k_near.append(along_z(k_own[1]))
    v_far = along_z(v_near)
    qshape = jax.ShapeDtypeStruct((kv_heads // 2, 2 * tokens, head_dim), jnp.bfloat16)
    k_near[1], k_near[0], v_near = hold((k_near[1], k_near[0], v_near))
    v_near_o, k_near_o = swap(v_near), [swap(k_near[0])]
    qs = call(prep_queries, (qshape, qshape), (queries_raw[0], qg, cosd, sind))
    state = (y0, y1, x1, k_own, k_near, v_near, v_far, list(qs), v_near_o, k_near_o)
    y0, y1, x1, k_own, k_near, v_near, v_far, qs, v_near_o, k_near_o = hold(state)

    y2 = move(y0, y_out)
    x2 = move(choose(flag, x1, y1), x_to)
    k_far = [along_z(k) for k in k_near]
    k_near_o.append(swap(k_near[1]))
    v_far_o = swap(v_far)
    k_far = hold(k_far)
    k_far_o = [swap(k_far[0])]

    def attention(i):
        return call(
            functools.partial(attend, i * kv_cols // 2),
            jax.ShapeDtypeStruct((kv_heads // 2, tokens, 2 * head_dim), jnp.bfloat16),
            (
                qs[i], lb,
                k_own[i], k_near[i], k_near_o[i], k_far[i], k_far_o[i], k_own_o[i],
                v_own, v_near, v_near_o, v_far, v_far_o, v_own_o,
            ),
            scalars=(info,),
            scratch=(pltpu.VMEM((tokens, kv_cols // 2), jnp.bfloat16),) * 2,
            limit=14,
        )

    att = [attention(0)]
    state = (y2, x1, x2, k_near, k_far, k_near_o, v_far, v_far_o, att)
    y2, x1, x2, k_near, k_far, k_near_o, v_far, v_far_o, att = hold(state)

    y3 = move(choose(flag, x1, x2), y_out)
    x3 = move(x2, x_to)
    k_far_o.append(swap(k_far[1]))
    att_o = [swap(att[0])]
    att.append(attention(1))
    att_o.append(swap(att[1]))

    g, y = fsdp // n_y, fsdp % n_y
    back = jnp.where(core == 0, -1, 1)
    first, second = (y + back) % n_y, (y - back) % n_y
    across_y = (y + 2) % n_y
    here, there = g * n_y, (1 - g) * n_y
    shards = [fsdp, here + first, here + second, here + across_y, there + y]
    shards += [there + jnp.where(same, first, y), there + jnp.where(same, second, first)]
    shards += [there + across_y, there + second]
    where = jnp.stack([core, dp, *shards]).astype(jnp.int32)

    n_tiles = 3
    tile = half_cols // n_tiles
    smem = pl.BlockSpec(memory_space=pltpu.SMEM)
    whole = pl.BlockSpec((kv_heads // 2, tokens, 2 * head_dim), lambda i: (0, 0, 0))
    column = pl.BlockSpec((rows, tile), lambda i: (0, i))
    double = pl.BlockSpec((2 * tokens, tile), lambda i: (0, i))
    heads = pltpu.VMEM((kv_heads, 2 * tokens, 2 * head_dim), jnp.bfloat16)
    params = pltpu.CompilerParams(vmem_limit_bytes=24 * MIB)
    early = pl.pallas_call(
        project_early,
        grid=(n_tiles,),
        out_shape=jax.ShapeDtypeStruct((2 * tokens, half_cols), f32),
        in_specs=[smem] + [whole] * 4 + [column] * 7,
        out_specs=double,
        scratch_shapes=[heads],
        compiler_params=params,
        cost_estimate=COST,
    )(where, *att, *att_o, own, y0, y1, y2, x0, x1, x2)
    y3, x3, early = hold((y3, x3, early))

    keep, send, sums, send_sums = pl.pallas_call(
        project_late,
        grid=(n_tiles,),
        out_shape=(
            jax.ShapeDtypeStruct((tokens, half_cols), jnp.bfloat16),
            jax.ShapeDtypeStruct((tokens, half_cols), jnp.bfloat16),
            jax.ShapeDtypeStruct((tokens, 128), f32),
            jax.ShapeDtypeStruct((tokens, 128), f32),
        ),
        in_specs=[smem] + [whole] * 4 + [double, column, column],
        out_specs=(
            pl.BlockSpec((tokens, tile), lambda i: (0, i)),
            pl.BlockSpec((tokens, tile), lambda i: (0, i)),
            pl.BlockSpec((tokens, 128), lambda i: (0, 0)),
            pl.BlockSpec((tokens, 128), lambda i: (0, 0)),
        ),
        scratch_shapes=[heads],
        compiler_params=params,
        cost_estimate=COST,
    )(where, *att, *att_o, early, y3, x3)
    came, came_sums = swap(send), swap(send_sums)
    n_rows = tokens // 4
    out = pl.pallas_call(
        norm_rows,
        grid=(4,),
        out_shape=jax.ShapeDtypeStruct((tokens, 2 * half_cols), jnp.bfloat16),
        in_specs=[smem]
        + [pl.BlockSpec((n_rows, half_cols), lambda i: (i, 0))] * 2
        + [pl.BlockSpec((n_rows, 128), lambda i: (i, 0))] * 2
        + [pl.BlockSpec((1, 2 * half_cols), lambda i: (0, 0))],
        out_specs=pl.BlockSpec((n_rows, 2 * half_cols), lambda i: (i, 0)),
        compiler_params=params,
        cost_estimate=COST,
    )(where, keep, came, sums, came_sums, post_gain[None, :])
    return out[None]


def solution(mesh):
    in_specs = (
        P(("dp", "fsdp"), "seq", None),
        P(("dp", "fsdp"), "seq", None),
        P(("dp", "fsdp"), None),
        P(),
        P(),
        P("fsdp", None),
        P(),
    )
    out_specs = P(("dp", "fsdp"), "seq", None)
    return jax.shard_map(
        on_device, mesh=mesh, in_specs=in_specs, out_specs=out_specs, check_vma=False
    )
```

```python
import functools
import math

import jax
import jax.numpy as jnp
from jax import lax
from jax.experimental import pallas as pl
from jax.experimental.pallas import tpu as pltpu
from jax.sharding import PartitionSpec as P

WINDOW = 1024
NEG = -1e30
attn_scale = 168.0 ** (-0.5)
norm_eps = 1e-06
SCORE_MUL = attn_scale * math.log2(math.e)
MIB = 1024 * 1024
COST = pl.CostEstimate(flops=10**6, bytes_accessed=10**4, transcendentals=0)


def vmem(n):
    return [pl.BlockSpec(memory_space=pltpu.VMEM)] * n


def call(body, out_shape, args, scalars=(), scratch=(), limit=8):
    specs = [pl.BlockSpec(memory_space=pltpu.SMEM)] * len(scalars) + vmem(len(args))
    return pl.pallas_call(
        body,
        out_shape=out_shape,
        in_specs=specs,
        out_specs=jax.tree.map(lambda _: pl.BlockSpec(memory_space=pltpu.VMEM), out_shape),
        scratch_shapes=list(scratch),
        compiler_params=pltpu.CompilerParams(vmem_limit_bytes=limit * MIB),
        cost_estimate=COST,
    )(*scalars, *args)


def choose_kernel(flag, a_ref, b_ref, out_ref, sem):
    @pl.when(flag[0] != 0)
    def _():
        copy = pltpu.make_async_copy(a_ref, out_ref, sem)
        copy.start()
        copy.wait()

    @pl.when(flag[0] == 0)
    def _():
        copy = pltpu.make_async_copy(b_ref, out_ref, sem)
        copy.start()
        copy.wait()


def choose(flag, a, b):
    anywhere = pl.BlockSpec(memory_space=pl.ANY)
    return pl.pallas_call(
        choose_kernel,
        out_shape=jax.ShapeDtypeStruct(a.shape, a.dtype),
        in_specs=[pl.BlockSpec(memory_space=pltpu.SMEM), anywhere, anywhere],
        out_specs=pl.BlockSpec(memory_space=pltpu.VMEM),
        scratch_shapes=[pltpu.SemaphoreType.DMA],
        compiler_params=pltpu.CompilerParams(vmem_limit_bytes=4 * MIB),
        cost_estimate=COST,
    )(flag, a, b)


def rope_head(x, gain, cosd, sind):
    x = x.astype(jnp.float32)
    meansq = jnp.mean(x * x, axis=-1, keepdims=True)
    y = x * lax.rsqrt(meansq + norm_eps) * gain
    half = y.shape[-1] // 2
    rolled = jnp.concatenate([y[:, half:], y[:, :half]], axis=-1)
    return (y * cosd + rolled * sind).astype(jnp.bfloat16)


def prep_keys(kv_ref, gain_ref, cos_ref, sin_ref, k0_ref, k1_ref):
    hd = gain_ref.shape[1]
    part = k0_ref.shape[1]
    for i, out in enumerate((k0_ref, k1_ref)):
        for at in range(0, part, hd):
            out[:, at : at + hd] = rope_head(
                kv_ref[:, i * part + at : i * part + at + hd], gain_ref[...], cos_ref[...], sin_ref[...]
            )


def prep_queries(q_ref, gain_ref, cos_ref, sin_ref, q0_ref, q1_ref):
    hd = gain_ref.shape[1]
    tokens = q_ref.shape[0]
    n = q_ref.shape[1] // hd // 2
    for h in range(2 * n):
        out = (q0_ref, q1_ref)[h // n]
        out[h % n // 2, (h % 2) * tokens : (h % 2 + 1) * tokens, :] = rope_head(
            q_ref[:, h * hd : (h + 1) * hd], gain_ref[...], cos_ref[...], sin_ref[...]
        )


def attend(info, q_ref, lb_ref, *refs):
    keys, values = refs[:6], refs[6:12]
    out_ref, k_rest, v_rest = refs[12:]
    tokens = keys[0].shape[0]
    hd = q_ref.shape[2]
    begin, core = info[0], info[1]

    @pl.when(core == 0)
    def _():
        k_rest[...] = keys[4][...]
        v_rest[...] = values[4][...]

    @pl.when(core != 0)
    def _():
        k_rest[...] = keys[5][...]
        v_rest[...] = values[5][...]

    lb = jnp.concatenate([lb_ref[...], lb_ref[...]], axis=0)
    rows = lax.broadcasted_iota(jnp.int32, (2 * tokens, tokens), 0)
    cols = lax.broadcasted_iota(jnp.int32, (2 * tokens, tokens), 1)
    ones = jnp.ones((tokens, hd), jnp.bfloat16)
    blocks = (
        (keys[0], values[0], begin),
        (keys[1], values[1], begin - 2 * tokens),
        (keys[2], values[2], begin - jnp.where(core == 0, 1, 3) * tokens),
        (k_rest, v_rest, begin - jnp.where(core == 0, 3, 1) * tokens),
        (keys[3], values[3], begin - 4 * tokens),
    )
    causal = cols <= lax.rem(rows, tokens)
    for j in range(out_ref.shape[0]):
        at = j * hd
        q = q_ref[j]
        scores = []
        for i, (k, _, base) in enumerate(blocks):
            s = lax.dot_general(
                q, k[:, at : at + hd], (((1,), (1,)), ((), ())), preferred_element_type=jnp.float32
            )
            keep = cols >= lb - base
            if i == 0:
                keep = keep & causal
            scores.append(jnp.where(keep, s * SCORE_MUL, NEG))
        top = functools.reduce(jnp.maximum, scores)
        top = jnp.max(top, axis=-1, keepdims=True)
        acc = jnp.zeros((2 * tokens, 2 * hd), jnp.float32)
        for s, (_, values_ref, _) in zip(scores, blocks):
            v = values_ref[:, at : at + hd]
            acc += jnp.dot(
                jnp.exp2(s - top).astype(jnp.bfloat16),
                jnp.concatenate([v, ones], axis=1),
                preferred_element_type=jnp.float32,
            )
        mixed = (acc[:, :hd] / acc[:, hd:]).astype(jnp.bfloat16)
        out_ref[j, :, :hd] = mixed[:tokens]
        out_ref[j, :, hd:] = mixed[tokens:]


def gather_heads(mine, other, att_ref):
    @pl.when(pl.program_id(0) == 0)
    def _():
        n, tokens = mine[0].shape[:2]
        for i in range(2):
            att_ref[i * n : (i + 1) * n, :tokens] = mine[i][...]
            att_ref[i * n : (i + 1) * n, tokens:] = other[i][...]


def multiply(items, extra, use_extra, info, att_ref, store):
    def run(items):
        wide = items[0][0].shape[1]
        for lo in range(0, wide, 256):
            hi = min(lo + 256, wide)
            total = None
            for ref, at in items:
                x = jnp.dot(att_ref[info[at]], ref[:, lo:hi], preferred_element_type=jnp.float32)
                total = x if total is None else total + x
            store(lo, hi, total)

    @pl.when(use_extra)
    def _():
        run(items + [extra])

    @pl.when(jnp.logical_not(use_extra))
    def _():
        run(items)


def project_early(info, m0, m1, o0, o1, own, y0, y1, y2, x0, x1, x2, acc_ref, att_ref):
    gather_heads((m0, m1), (o0, o1), att_ref)

    def store(lo, hi, total):
        acc_ref[:, lo:hi] = total

    items = [(own, 2), (y0, 3), (y1, 4), (y2, 5), (x1, 7), (x2, 8)]
    multiply(items, (x0, 6), info[0] == info[1], info, att_ref, store)


def project_late(info, m0, m1, o0, o1, early_ref, y3, x3, keep_ref, send_ref, *rest):
    sums, att_ref = rest[:2], rest[2]
    gather_heads((m0, m1), (o0, o1), att_ref)
    tokens = keep_ref.shape[0]

    @pl.when(pl.program_id(0) == 0)
    def _():
        for ref in sums:
            ref[...] = jnp.zeros_like(ref)

    def store(lo, hi, total):
        total = total + early_ref[:, lo:hi]
        keep_ref[:, lo:hi] = total[:tokens].astype(jnp.bfloat16)
        send_ref[:, lo:hi] = total[tokens:].astype(jnp.bfloat16)
        for i, ref in enumerate(sums):
            squares = ref[...]
            for at in range(0, hi - lo, 128):
                x = total[i * tokens : (i + 1) * tokens, at : at + 128]
                squares += x * x
            ref[...] = squares

    multiply([(y3, 9)], (x3, 10), info[0] != info[1], info, att_ref, store)


def norm_rows(info, keep_ref, came_ref, sum_ref, came_sum_ref, gain_ref, out_ref):
    half = keep_ref.shape[1]
    squares = jnp.sum(sum_ref[...] + came_sum_ref[...], axis=-1, keepdims=True)
    scale = lax.rsqrt(squares / (2 * half) + norm_eps)

    def write(at, ref):
        out_ref[:, at : at + half] = (
            ref[...].astype(jnp.float32) * scale * gain_ref[:, at : at + half]
        ).astype(jnp.bfloat16)

    for core in range(2):

        @pl.when(info[0] == core)
        def _():
            write(core * half, keep_ref)
            write((1 - core) * half, came_ref)


def on_device(queries_raw, keys_values, doc_ids, q_gain, k_gain, out_weight, post_gain):
    tokens, feat = queries_raw.shape[1:]
    head_dim = q_gain.shape[0]
    kv_cols = keys_values.shape[2] // 2
    kv_heads = kv_cols // head_dim
    n_seq = lax.axis_size("seq")
    n_fsdp = lax.axis_size("fsdp")
    n_y = n_fsdp // 2
    seq, fsdp, dp = lax.axis_index("seq"), lax.axis_index("fsdp"), lax.axis_index("dp")
    core = lax.rem(seq, 2)
    begin = seq * tokens
    f32 = jnp.float32

    forward = [(i, (i + 2) % n_seq) for i in range(n_seq)]
    across = [(i, i ^ 1) for i in range(n_seq)]
    everywhere = ("dp", "seq", "fsdp")

    def route(to):
        out = []
        for d in range(2):
            for q in range(n_seq):
                for f in range(n_fsdp):
                    e, r, g = to(d, q, f)
                    out.append(((d * n_seq + q) * n_fsdp + f, (e * n_seq + r) * n_fsdp + g))
        return out

    def turn(f, step):
        return f // n_y * n_y + (f + step) % n_y

    def y_out(d, q, f):
        return d, q, turn(f, -1 if q % 2 else 1)

    def y_back(d, q, f):
        return d, q, turn(f, 1 if q % 2 else -1)

    def x_to(d, q, f):
        return 1 - d, q, f if q % 2 == d else (f + n_y) % n_fsdp

    def move(x, to):
        return lax.ppermute(x, everywhere, route(to))

    def along_z(x):
        return lax.ppermute(x, "seq", forward)

    def swap(x):
        return lax.ppermute(x, "seq", across)

    ids = doc_ids[0]
    my_ids = lax.dynamic_slice_in_dim(ids, begin, tokens, 0)
    token = begin + jnp.arange(tokens, dtype=jnp.int32)
    start = jnp.sum((ids[None, :] < my_ids[:, None]).astype(jnp.int32), axis=1)
    positions = token - start
    lb = jnp.maximum(start, token - (WINDOW - 1))[:, None]
    half = head_dim // 2
    inverse = 10000.0 ** (-(jnp.arange(half, dtype=f32) * 2.0 / head_dim))
    angles = positions.astype(f32)[:, None] * inverse[None, :]
    cosine, sine = jnp.cos(angles), jnp.sin(angles)
    cosd = jnp.concatenate([cosine, cosine], axis=1)
    sind = jnp.concatenate([-sine, sine], axis=1)
    kg, qg = k_gain[None, :], q_gain[None, :]

    raw = keys_values[0]
    half_cols = out_weight.shape[1] // 2
    rows = out_weight.shape[0]
    hold = lax.optimization_barrier
    info = jnp.stack([begin, core]).astype(jnp.int32)
    same = core == dp
    flag = same.astype(jnp.int32)[None]

    own = lax.dynamic_slice(out_weight, (0, core * half_cols), (rows, half_cols))
    y0 = move(own, y_out)
    x0 = move(own, x_to)
    raw, own = hold((raw, own))
    part = kv_cols // 2
    v_own = [raw[:, kv_cols : kv_cols + part], raw[:, kv_cols + part :]]
    v_near = [along_z(v) for v in v_own]
    shape = jax.ShapeDtypeStruct((tokens, part), jnp.bfloat16)
    k_own = call(prep_keys, (shape, shape), (raw, kg, cosd, sind))
    k_near = [along_z(k_own[0])]
    qshape = jax.ShapeDtypeStruct((kv_heads // 2, 2 * tokens, head_dim), jnp.bfloat16)
    qs = call(prep_queries, (qshape, qshape), (queries_raw[0], qg, cosd, sind))
    state = (y0, x0, own, v_own, v_near, list(k_own), k_near, list(qs))
    y0, x0, own, v_own, v_near, k_own, k_near, qs = hold(state)

    y1 = move(own, y_back)
    x1 = move(choose(flag, x0, y0), x_to)
    k_near.append(along_z(k_own[1]))
    k_far, v_far = [along_z(k_near[0])], [along_z(v_near[0])]
    k_near, v_near, k_own, v_own = hold((k_near, v_near, k_own, v_own))
    k_own_o, v_own_o, k_near_o, v_near_o = ([swap(x[0])] for x in (k_own, v_own, k_near, v_near))
    state = (y0, y1, x1, k_own, v_own, k_near, v_near, k_far, v_far, k_own_o, v_own_o, k_near_o, v_near_o)
    y0, y1, x1, k_own, v_own, k_near, v_near, k_far, v_far, k_own_o, v_own_o, k_near_o, v_near_o = hold(state)

    y2 = move(y0, y_out)
    x2 = move(choose(flag, x1, y1), x_to)
    k_far.append(along_z(k_near[1]))
    v_far.append(along_z(v_near[1]))
    k_far_o, v_far_o = [swap(k_far[0])], [swap(v_far[0])]

    def attention(i):
        return call(
            attend,
            jax.ShapeDtypeStruct((kv_heads // 2, tokens, 2 * head_dim), jnp.bfloat16),
            (
                qs[i], lb,
                k_own[i], k_near[i], k_near_o[i], k_far[i], k_far_o[i], k_own_o[i],
                v_own[i], v_near[i], v_near_o[i], v_far[i], v_far_o[i], v_own_o[i],
            ),
            scalars=(info,),
            scratch=(pltpu.VMEM((tokens, kv_cols // 2), jnp.bfloat16),) * 2,
            limit=60,
        )

    att = [attention(0)]
    k_own, v_own, k_near, v_near, k_far[1], v_far[1], att = hold((k_own, v_own, k_near, v_near, k_far[1], v_far[1], att))
    for have, came in ((k_own, k_own_o), (v_own, v_own_o), (k_near, k_near_o), (v_near, v_near_o)):
        came.append(swap(have[1]))
    k_far_o.append(swap(k_far[1]))
    v_far_o.append(swap(v_far[1]))
    state = (y2, x1, x2, k_far, v_far, att, k_own_o, v_own_o, k_near_o, v_near_o, k_far_o, v_far_o)
    y2, x1, x2, k_far, v_far, att, k_own_o, v_own_o, k_near_o, v_near_o, k_far_o, v_far_o = hold(state)

    y3 = move(choose(flag, x1, x2), y_out)
    x3 = move(x2, x_to)
    att_o = [swap(att[0])]
    att.append(attention(1))
    att_o.append(swap(att[1]))

    g, y = fsdp // n_y, fsdp % n_y
    back = jnp.where(core == 0, -1, 1)
    first, second = (y + back) % n_y, (y - back) % n_y
    across_y = (y + 2) % n_y
    here, there = g * n_y, (1 - g) * n_y
    shards = [fsdp, here + first, here + second, here + across_y, there + y]
    shards += [there + jnp.where(same, first, y), there + jnp.where(same, second, first)]
    shards += [there + across_y, there + second]
    where = jnp.stack([core, dp, *shards]).astype(jnp.int32)

    n_tiles = 3
    tile = half_cols // n_tiles
    smem = pl.BlockSpec(memory_space=pltpu.SMEM)
    whole = pl.BlockSpec((kv_heads // 2, tokens, 2 * head_dim), lambda i: (0, 0, 0))
    column = pl.BlockSpec((rows, tile), lambda i: (0, i))
    double = pl.BlockSpec((2 * tokens, tile), lambda i: (0, i))
    heads = pltpu.VMEM((kv_heads, 2 * tokens, 2 * head_dim), jnp.bfloat16)
    params = pltpu.CompilerParams(vmem_limit_bytes=24 * MIB)
    early = pl.pallas_call(
        project_early,
        grid=(n_tiles,),
        out_shape=jax.ShapeDtypeStruct((2 * tokens, half_cols), f32),
        in_specs=[smem] + [whole] * 4 + [column] * 7,
        out_specs=double,
        scratch_shapes=[heads],
        compiler_params=params,
        cost_estimate=COST,
    )(where, *att, *att_o, own, y0, y1, y2, x0, x1, x2)
    y3, x3, early = hold((y3, x3, early))

    keep, send, sums, send_sums = pl.pallas_call(
        project_late,
        grid=(n_tiles,),
        out_shape=(
            jax.ShapeDtypeStruct((tokens, half_cols), jnp.bfloat16),
            jax.ShapeDtypeStruct((tokens, half_cols), jnp.bfloat16),
            jax.ShapeDtypeStruct((tokens, 128), f32),
            jax.ShapeDtypeStruct((tokens, 128), f32),
        ),
        in_specs=[smem] + [whole] * 4 + [double, column, column],
        out_specs=(
            pl.BlockSpec((tokens, tile), lambda i: (0, i)),
            pl.BlockSpec((tokens, tile), lambda i: (0, i)),
            pl.BlockSpec((tokens, 128), lambda i: (0, 0)),
            pl.BlockSpec((tokens, 128), lambda i: (0, 0)),
        ),
        scratch_shapes=[heads],
        compiler_params=params,
        cost_estimate=COST,
    )(where, *att, *att_o, early, y3, x3)
    came, came_sums = swap(send), swap(send_sums)
    n_rows = tokens // 4
    out = pl.pallas_call(
        norm_rows,
        grid=(4,),
        out_shape=jax.ShapeDtypeStruct((tokens, 2 * half_cols), jnp.bfloat16),
        in_specs=[smem]
        + [pl.BlockSpec((n_rows, half_cols), lambda i: (i, 0))] * 2
        + [pl.BlockSpec((n_rows, 128), lambda i: (i, 0))] * 2
        + [pl.BlockSpec((1, 2 * half_cols), lambda i: (0, 0))],
        out_specs=pl.BlockSpec((n_rows, 2 * half_cols), lambda i: (i, 0)),
        compiler_params=params,
        cost_estimate=COST,
    )(where, keep, came, sums, came_sums, post_gain[None, :])
    return out[None]


def solution(mesh):
    in_specs = (
        P(("dp", "fsdp"), "seq", None),
        P(("dp", "fsdp"), "seq", None),
        P(("dp", "fsdp"), None),
        P(),
        P(),
        P("fsdp", None),
        P(),
    )
    out_specs = P(("dp", "fsdp"), "seq", None)
    return jax.shard_map(
        on_device, mesh=mesh, in_specs=in_specs, out_specs=out_specs, check_vma=False
    )
```

```python
import functools
import math

import jax
import jax.numpy as jnp
from jax import lax
from jax.experimental import pallas as pl
from jax.experimental.pallas import tpu as pltpu
from jax.sharding import PartitionSpec as P

WINDOW = 1024
NEG = -1e30
attn_scale = 168.0 ** (-0.5)
norm_eps = 1e-06
SCORE_MUL = attn_scale * math.log2(math.e)
MIB = 1024 * 1024
COST = pl.CostEstimate(flops=10**6, bytes_accessed=10**4, transcendentals=0)


def vmem(n):
    return [pl.BlockSpec(memory_space=pltpu.VMEM)] * n


def call(body, out_shape, args, scalars=(), scratch=(), limit=8):
    specs = [pl.BlockSpec(memory_space=pltpu.SMEM)] * len(scalars) + vmem(len(args))
    return pl.pallas_call(
        body,
        out_shape=out_shape,
        in_specs=specs,
        out_specs=jax.tree.map(lambda _: pl.BlockSpec(memory_space=pltpu.VMEM), out_shape),
        scratch_shapes=list(scratch),
        compiler_params=pltpu.CompilerParams(vmem_limit_bytes=limit * MIB),
        cost_estimate=COST,
    )(*scalars, *args)


def choose_kernel(flag, a_ref, b_ref, out_ref, sem):
    @pl.when(flag[0] != 0)
    def _():
        copy = pltpu.make_async_copy(a_ref, out_ref, sem)
        copy.start()
        copy.wait()

    @pl.when(flag[0] == 0)
    def _():
        copy = pltpu.make_async_copy(b_ref, out_ref, sem)
        copy.start()
        copy.wait()


def choose(flag, a, b):
    anywhere = pl.BlockSpec(memory_space=pl.ANY)
    return pl.pallas_call(
        choose_kernel,
        out_shape=jax.ShapeDtypeStruct(a.shape, a.dtype),
        in_specs=[pl.BlockSpec(memory_space=pltpu.SMEM), anywhere, anywhere],
        out_specs=pl.BlockSpec(memory_space=pltpu.VMEM),
        scratch_shapes=[pltpu.SemaphoreType.DMA],
        compiler_params=pltpu.CompilerParams(vmem_limit_bytes=4 * MIB),
        cost_estimate=COST,
    )(flag, a, b)


def rope_head(x, gain, cosd, sind):
    x = x.astype(jnp.float32)
    meansq = jnp.mean(x * x, axis=-1, keepdims=True)
    y = x * lax.rsqrt(meansq + norm_eps) * gain
    half = y.shape[-1] // 2
    rolled = jnp.concatenate([y[:, half:], y[:, :half]], axis=-1)
    return (y * cosd + rolled * sind).astype(jnp.bfloat16)


def prep_keys(kv_ref, gain_ref, cos_ref, sin_ref, k0_ref, k1_ref):
    hd = gain_ref.shape[1]
    part = k0_ref.shape[1]
    for i, out in enumerate((k0_ref, k1_ref)):
        for at in range(0, part, hd):
            out[:, at : at + hd] = rope_head(
                kv_ref[:, i * part + at : i * part + at + hd], gain_ref[...], cos_ref[...], sin_ref[...]
            )


def prep_queries(q_ref, gain_ref, cos_ref, sin_ref, q0_ref, q1_ref):
    hd = gain_ref.shape[1]
    tokens = q_ref.shape[0]
    n = q_ref.shape[1] // hd // 2
    for h in range(2 * n):
        out = (q0_ref, q1_ref)[h // n]
        out[h % n // 2, (h % 2) * tokens : (h % 2 + 1) * tokens, :] = rope_head(
            q_ref[:, h * hd : (h + 1) * hd], gain_ref[...], cos_ref[...], sin_ref[...]
        )


def attend(info, q_ref, lb_ref, *refs):
    keys, values = refs[:6], refs[6:12]
    out_ref, k_rest, v_rest = refs[12:]
    tokens = keys[0].shape[0]
    hd = q_ref.shape[2]
    begin, core = info[0], info[1]

    @pl.when(core == 0)
    def _():
        k_rest[...] = keys[4][...]
        v_rest[...] = values[4][...]

    @pl.when(core != 0)
    def _():
        k_rest[...] = keys[5][...]
        v_rest[...] = values[5][...]

    lb = jnp.concatenate([lb_ref[...], lb_ref[...]], axis=0)
    rows = lax.broadcasted_iota(jnp.int32, (2 * tokens, tokens), 0)
    cols = lax.broadcasted_iota(jnp.int32, (2 * tokens, tokens), 1)
    ones = jnp.ones((tokens, hd), jnp.bfloat16)
    blocks = (
        (keys[1], values[1], begin - 2 * tokens),
        (keys[2], values[2], begin - jnp.where(core == 0, 1, 3) * tokens),
        (k_rest, v_rest, begin - jnp.where(core == 0, 3, 1) * tokens),
    )
    causal = cols <= lax.rem(rows, tokens)
    edge = jnp.where(causal, cols, cols - WINDOW)

    def product(q, k):
        return lax.dot_general(q, k, (((1,), (1,)), ((), ())), preferred_element_type=jnp.float32)

    def weigh(p, v):
        return jnp.dot(
            p.astype(jnp.bfloat16), jnp.concatenate([v, ones], axis=1), preferred_element_type=jnp.float32
        )

    for j in range(out_ref.shape[0]):
        head = slice(j * hd, (j + 1) * hd)
        q = q_ref[j]
        s = jnp.where(causal, product(q, keys[0][:, head]), product(q, keys[3][:, head]))
        scores = [jnp.where(edge >= lb - begin, s * SCORE_MUL, NEG)]
        for k, _, base in blocks:
            scores.append(jnp.where(cols >= lb - base, product(q, k[:, head]) * SCORE_MUL, NEG))
        top = functools.reduce(jnp.maximum, scores)
        top = jnp.max(top, axis=-1, keepdims=True)
        p = jnp.exp2(scores[0] - top)
        acc = weigh(jnp.where(causal, p, 0.0), values[0][:, head])
        acc += weigh(jnp.where(causal, 0.0, p), values[3][:, head])
        for s, (_, v, _) in zip(scores[1:], blocks):
            acc += weigh(jnp.exp2(s - top), v[:, head])
        mixed = (acc[:, :hd] / acc[:, hd:]).astype(jnp.bfloat16)
        out_ref[j, :, :hd] = mixed[:tokens]
        out_ref[j, :, hd:] = mixed[tokens:]


def gather_heads(mine, other, att_ref):
    @pl.when(pl.program_id(0) == 0)
    def _():
        n, tokens = mine[0].shape[:2]
        for i in range(2):
            att_ref[i * n : (i + 1) * n, :tokens] = mine[i][...]
            att_ref[i * n : (i + 1) * n, tokens:] = other[i][...]


def multiply(items, extra, use_extra, info, att_ref, store):
    def run(items):
        wide = items[0][0].shape[1]
        for lo in range(0, wide, 256):
            hi = min(lo + 256, wide)
            total = None
            for ref, at in items:
                x = jnp.dot(att_ref[info[at]], ref[:, lo:hi], preferred_element_type=jnp.float32)
                total = x if total is None else total + x
            store(lo, hi, total)

    @pl.when(use_extra)
    def _():
        run(items + [extra])

    @pl.when(jnp.logical_not(use_extra))
    def _():
        run(items)


def project_early(info, m0, m1, o0, o1, own, y0, y1, y2, x0, x1, x2, acc_ref, att_ref):
    gather_heads((m0, m1), (o0, o1), att_ref)

    def store(lo, hi, total):
        acc_ref[:, lo:hi] = total

    items = [(own, 2), (y0, 3), (y1, 4), (y2, 5), (x1, 7), (x2, 8)]
    multiply(items, (x0, 6), info[0] == info[1], info, att_ref, store)


def project_late(info, m0, m1, o0, o1, early_ref, y3, x3, keep_ref, send_ref, *rest):
    sums, att_ref = rest[:2], rest[2]
    gather_heads((m0, m1), (o0, o1), att_ref)
    tokens = keep_ref.shape[0]

    @pl.when(pl.program_id(0) == 0)
    def _():
        for ref in sums:
            ref[...] = jnp.zeros_like(ref)

    def store(lo, hi, total):
        total = total + early_ref[:, lo:hi]
        keep_ref[:, lo:hi] = total[:tokens].astype(jnp.bfloat16)
        send_ref[:, lo:hi] = total[tokens:].astype(jnp.bfloat16)
        for i, ref in enumerate(sums):
            squares = ref[...]
            for at in range(0, hi - lo, 128):
                x = total[i * tokens : (i + 1) * tokens, at : at + 128]
                squares += x * x
            ref[...] = squares

    multiply([(y3, 9)], (x3, 10), info[0] != info[1], info, att_ref, store)


def norm_rows(info, keep_ref, came_ref, sum_ref, came_sum_ref, gain_ref, out_ref):
    half = keep_ref.shape[1]
    squares = jnp.sum(sum_ref[...] + came_sum_ref[...], axis=-1, keepdims=True)
    scale = lax.rsqrt(squares / (2 * half) + norm_eps)

    def write(at, ref):
        out_ref[:, at : at + half] = (
            ref[...].astype(jnp.float32) * scale * gain_ref[:, at : at + half]
        ).astype(jnp.bfloat16)

    for core in range(2):

        @pl.when(info[0] == core)
        def _():
            write(core * half, keep_ref)
            write((1 - core) * half, came_ref)


def on_device(queries_raw, keys_values, doc_ids, q_gain, k_gain, out_weight, post_gain):
    tokens, feat = queries_raw.shape[1:]
    head_dim = q_gain.shape[0]
    kv_cols = keys_values.shape[2] // 2
    kv_heads = kv_cols // head_dim
    n_seq = lax.axis_size("seq")
    n_fsdp = lax.axis_size("fsdp")
    n_y = n_fsdp // 2
    seq, fsdp, dp = lax.axis_index("seq"), lax.axis_index("fsdp"), lax.axis_index("dp")
    core = lax.rem(seq, 2)
    begin = seq * tokens
    f32 = jnp.float32

    forward = [(i, (i + 2) % n_seq) for i in range(n_seq)]
    across = [(i, i ^ 1) for i in range(n_seq)]
    everywhere = ("dp", "seq", "fsdp")

    def route(to):
        out = []
        for d in range(2):
            for q in range(n_seq):
                for f in range(n_fsdp):
                    e, r, g = to(d, q, f)
                    out.append(((d * n_seq + q) * n_fsdp + f, (e * n_seq + r) * n_fsdp + g))
        return out

    def turn(f, step):
        return f // n_y * n_y + (f + step) % n_y

    def y_out(d, q, f):
        return d, q, turn(f, -1 if q % 2 else 1)

    def y_back(d, q, f):
        return d, q, turn(f, 1 if q % 2 else -1)

    def x_to(d, q, f):
        return 1 - d, q, f if q % 2 == d else (f + n_y) % n_fsdp

    def move(x, to):
        return lax.ppermute(x, everywhere, route(to))

    def along_z(x):
        return lax.ppermute(x, "seq", forward)

    def swap(x):
        return lax.ppermute(x, "seq", across)

    ids = doc_ids[0]
    my_ids = lax.dynamic_slice_in_dim(ids, begin, tokens, 0)
    token = begin + jnp.arange(tokens, dtype=jnp.int32)
    start = jnp.sum((ids[None, :] < my_ids[:, None]).astype(jnp.int32), axis=1)
    positions = token - start
    lb = jnp.maximum(start, token - (WINDOW - 1))[:, None]
    half = head_dim // 2
    inverse = 10000.0 ** (-(jnp.arange(half, dtype=f32) * 2.0 / head_dim))
    angles = positions.astype(f32)[:, None] * inverse[None, :]
    cosine, sine = jnp.cos(angles), jnp.sin(angles)
    cosd = jnp.concatenate([cosine, cosine], axis=1)
    sind = jnp.concatenate([-sine, sine], axis=1)
    kg, qg = k_gain[None, :], q_gain[None, :]

    raw = keys_values[0]
    half_cols = out_weight.shape[1] // 2
    rows = out_weight.shape[0]
    hold = lax.optimization_barrier
    info = jnp.stack([begin, core]).astype(jnp.int32)
    same = core == dp
    flag = same.astype(jnp.int32)[None]

    own = lax.dynamic_slice(out_weight, (0, core * half_cols), (rows, half_cols))
    y0 = move(own, y_out)
    x0 = move(own, x_to)
    raw, own = hold((raw, own))
    part = kv_cols // 2
    v_own = [raw[:, kv_cols : kv_cols + part], raw[:, kv_cols + part :]]
    v_near = [along_z(v) for v in v_own]
    shape = jax.ShapeDtypeStruct((tokens, part), jnp.bfloat16)
    k_own = call(prep_keys, (shape, shape), (raw, kg, cosd, sind))
    k_near = [along_z(k_own[0])]
    qshape = jax.ShapeDtypeStruct((kv_heads // 2, 2 * tokens, head_dim), jnp.bfloat16)
    qs = call(prep_queries, (qshape, qshape), (queries_raw[0], qg, cosd, sind))
    state = (y0, x0, own, v_own, v_near, list(k_own), k_near, list(qs))
    y0, x0, own, v_own, v_near, k_own, k_near, qs = hold(state)

    y1 = move(own, y_back)
    x1 = move(choose(flag, x0, y0), x_to)
    k_near.append(along_z(k_own[1]))
    k_far, v_far = [along_z(k_near[0])], [along_z(v_near[0])]
    k_near, v_near, k_own, v_own = hold((k_near, v_near, k_own, v_own))
    k_own_o, v_own_o, k_near_o, v_near_o = ([swap(x[0])] for x in (k_own, v_own, k_near, v_near))
    state = (y0, y1, x1, k_own, v_own, k_near, v_near, k_far, v_far, k_own_o, v_own_o, k_near_o, v_near_o)
    y0, y1, x1, k_own, v_own, k_near, v_near, k_far, v_far, k_own_o, v_own_o, k_near_o, v_near_o = hold(state)

    y2 = move(y0, y_out)
    x2 = move(choose(flag, x1, y1), x_to)
    k_far.append(along_z(k_near[1]))
    v_far.append(along_z(v_near[1]))
    k_far_o, v_far_o = [swap(k_far[0])], [swap(v_far[0])]

    def attention(i):
        return call(
            attend,
            jax.ShapeDtypeStruct((kv_heads // 2, tokens, 2 * head_dim), jnp.bfloat16),
            (
                qs[i], lb,
                k_own[i], k_near[i], k_near_o[i], k_far[i], k_far_o[i], k_own_o[i],
                v_own[i], v_near[i], v_near_o[i], v_far[i], v_far_o[i], v_own_o[i],
            ),
            scalars=(info,),
            scratch=(pltpu.VMEM((tokens, kv_cols // 2), jnp.bfloat16),) * 2,
            limit=60,
        )

    att = [attention(0)]
    k_own, v_own, k_near, v_near, k_far[1], v_far[1], att = hold((k_own, v_own, k_near, v_near, k_far[1], v_far[1], att))
    for have, came in ((k_own, k_own_o), (v_own, v_own_o), (k_near, k_near_o), (v_near, v_near_o)):
        came.append(swap(have[1]))
    k_far_o.append(swap(k_far[1]))
    v_far_o.append(swap(v_far[1]))
    state = (y2, x1, x2, k_far, v_far, att, k_own_o, v_own_o, k_near_o, v_near_o, k_far_o, v_far_o)
    y2, x1, x2, k_far, v_far, att, k_own_o, v_own_o, k_near_o, v_near_o, k_far_o, v_far_o = hold(state)

    y3 = move(choose(flag, x1, x2), y_out)
    x3 = move(x2, x_to)
    att_o = [swap(att[0])]
    att.append(attention(1))
    att_o.append(swap(att[1]))

    g, y = fsdp // n_y, fsdp % n_y
    back = jnp.where(core == 0, -1, 1)
    first, second = (y + back) % n_y, (y - back) % n_y
    across_y = (y + 2) % n_y
    here, there = g * n_y, (1 - g) * n_y
    shards = [fsdp, here + first, here + second, here + across_y, there + y]
    shards += [there + jnp.where(same, first, y), there + jnp.where(same, second, first)]
    shards += [there + across_y, there + second]
    where = jnp.stack([core, dp, *shards]).astype(jnp.int32)

    n_tiles = 3
    tile = half_cols // n_tiles
    smem = pl.BlockSpec(memory_space=pltpu.SMEM)
    whole = pl.BlockSpec((kv_heads // 2, tokens, 2 * head_dim), lambda i: (0, 0, 0))
    column = pl.BlockSpec((rows, tile), lambda i: (0, i))
    double = pl.BlockSpec((2 * tokens, tile), lambda i: (0, i))
    heads = pltpu.VMEM((kv_heads, 2 * tokens, 2 * head_dim), jnp.bfloat16)
    params = pltpu.CompilerParams(vmem_limit_bytes=24 * MIB)
    early = pl.pallas_call(
        project_early,
        grid=(n_tiles,),
        out_shape=jax.ShapeDtypeStruct((2 * tokens, half_cols), f32),
        in_specs=[smem] + [whole] * 4 + [column] * 7,
        out_specs=double,
        scratch_shapes=[heads],
        compiler_params=params,
        cost_estimate=COST,
    )(where, *att, *att_o, own, y0, y1, y2, x0, x1, x2)
    y3, x3, early = hold((y3, x3, early))

    keep, send, sums, send_sums = pl.pallas_call(
        project_late,
        grid=(n_tiles,),
        out_shape=(
            jax.ShapeDtypeStruct((tokens, half_cols), jnp.bfloat16),
            jax.ShapeDtypeStruct((tokens, half_cols), jnp.bfloat16),
            jax.ShapeDtypeStruct((tokens, 128), f32),
            jax.ShapeDtypeStruct((tokens, 128), f32),
        ),
        in_specs=[smem] + [whole] * 4 + [double, column, column],
        out_specs=(
            pl.BlockSpec((tokens, tile), lambda i: (0, i)),
            pl.BlockSpec((tokens, tile), lambda i: (0, i)),
            pl.BlockSpec((tokens, 128), lambda i: (0, 0)),
            pl.BlockSpec((tokens, 128), lambda i: (0, 0)),
        ),
        scratch_shapes=[heads],
        compiler_params=params,
        cost_estimate=COST,
    )(where, *att, *att_o, early, y3, x3)
    came, came_sums = swap(send), swap(send_sums)
    n_rows = tokens // 4
    out = pl.pallas_call(
        norm_rows,
        grid=(4,),
        out_shape=jax.ShapeDtypeStruct((tokens, 2 * half_cols), jnp.bfloat16),
        in_specs=[smem]
        + [pl.BlockSpec((n_rows, half_cols), lambda i: (i, 0))] * 2
        + [pl.BlockSpec((n_rows, 128), lambda i: (i, 0))] * 2
        + [pl.BlockSpec((1, 2 * half_cols), lambda i: (0, 0))],
        out_specs=pl.BlockSpec((n_rows, 2 * half_cols), lambda i: (i, 0)),
        compiler_params=params,
        cost_estimate=COST,
    )(where, keep, came, sums, came_sums, post_gain[None, :])
    return out[None]


def solution(mesh):
    in_specs = (
        P(("dp", "fsdp"), "seq", None),
        P(("dp", "fsdp"), "seq", None),
        P(("dp", "fsdp"), None),
        P(),
        P(),
        P("fsdp", None),
        P(),
    )
    out_specs = P(("dp", "fsdp"), "seq", None)
    return jax.shard_map(
        on_device, mesh=mesh, in_specs=in_specs, out_specs=out_specs, check_vma=False
    )
```
